32 devices in a mesh: ctx: 8 (over z, y), tp: 4 (over x, core).
Axes of the slice: x: 2, y: 2, z: 4, core: 2. Of those that a mesh axis runs over, the one named last changes fastest.
Arguments:
- block_q: bfloat16 [2048, 8192], P('ctx', 'tp'), may hold values from -200 to 200
- block_kv: bfloat16 [2, 2048, 1024], P(None, 'ctx', 'tp'), may hold values from -6 to 6
- lengths: int32 [8], P('ctx'), may hold values from 128 to 256, as said below
- tenant: int32 [1], replicated, may hold values from 0 to 7
- prefix_kv: bfloat16 [2, 8, 512, 1024], P(None, 'ctx', None, 'tp'), may hold values from -6 to 6
- decode_q: bfloat16 [2, 8, 8192], P(None, 'ctx', 'tp'), may hold values from -200 to 200
- decode_pos: int32 [2, 8], P(None, 'ctx'), may hold values from 513 to 2048
Outputs:
- prefill_out: bfloat16 [2048, 8192], P('ctx', 'tp')
- decode_out: bfloat16 [2, 8, 8192], P(None, 'ctx', 'tp')
The draws below stay inside these ranges and needn't reach their ends.
Inputs may be any that keep to these rules, and one draw needn't show every extreme that they name: The lengths sum to 1536.
All inputs are finite; a program needn't handle non-finite values.
Results may differ from the reference program's by a relative error of at most 0.007.
Values may be sent and summed in bfloat16 or wider, within the bound.
A program may use at most 320 MiB of HBM per device.

```python
import jax
import jax.numpy as jnp
from jax import lax

QH = 64
KVH = 8
HD = 128
BLK = 256
ANC = 512
STEPS = 2
BLOCKS = 8
TENANTS = 8
CONTEXT = 2048
QROWS = 8
VALID = 1536


def block_counts(key):
    key = jax.random.fold_in(key, 51)
    first_key, second_key = jax.random.split(key)
    half_count = BLOCKS // 2
    quarter = BLK // 4
    swing = jax.random.randint(first_key, (half_count,), 0, quarter + 1).astype(jnp.int32)
    swing = swing.at[0].set(quarter)
    values = jnp.concatenate([3 * quarter + swing, 3 * quarter - swing], 0).astype(jnp.int32)
    places = jax.random.permutation(second_key, BLOCKS)
    return jnp.zeros((BLOCKS,), jnp.int32).at[places].set(values)


def draw_lengths(key, part):
    counts = block_counts(key)
    return counts


def draw_block_q(key, part):
    key = jax.random.fold_in(key, 11)
    shape = (CONTEXT, QH * HD)
    return jnp.clip(3.0 * jax.random.normal(key, shape, jnp.float32), -12.0, 12.0).astype(jnp.bfloat16)


def draw_decode_q(key, part):
    key = jax.random.fold_in(key, 23)
    shape = (STEPS, QROWS, QH * HD)
    return jnp.clip(3.0 * jax.random.normal(key, shape, jnp.float32), -12.0, 12.0).astype(jnp.bfloat16)


def draw_decode_pos(key, part):
    counts = block_counts(key)
    key = jax.random.fold_in(key, 37)
    first_key, second_key = jax.random.split(key)
    flat_count = STEPS * QROWS
    starts = jnp.cumsum(counts) - counts
    middle = BLOCKS // 2
    middle_end = ANC + starts[middle] + counts[middle]
    before_end = ANC + starts[middle - 1] + counts[middle - 1]
    positions_flat = jax.random.randint(first_key, (flat_count,), ANC + 1, ANC + VALID + 1)
    places = jax.random.permutation(second_key, flat_count)
    first_group = max(flat_count // 4, 1)
    second_group = max(flat_count // 8, 1)
    positions_flat = positions_flat.at[places[2:2 + first_group]].set(middle_end)
    positions_flat = positions_flat.at[places[2 + first_group:2 + first_group + second_group]].set(before_end)
    positions_flat = positions_flat.at[places[0]].set(ANC + VALID)
    positions_flat = positions_flat.at[places[1]].set(ANC + 1)
    return positions_flat.astype(jnp.int32).reshape(STEPS, QROWS)


def steps_of(rng, dims, cuts, least, high):
    def one(dim, blocks):
        steps = jax.random.uniform(jax.random.fold_in(jax.random.fold_in(rng, 6), dim), (blocks,), jnp.float32, least / len(cuts), high / len(cuts))
        return jnp.repeat(jnp.exp(steps), dims[dim] // blocks).reshape((-1,) + (1,) * (len(dims) - dim - 1))

    factor_of = one(*cuts[0])
    for cut in cuts[1:]:
        factor_of = factor_of * one(*cut)
    return factor_of


def normal_values(own_key, shape, scale, bound, cuts=(), held_as=jnp.bfloat16):
    loudness = steps_of(own_key, shape, cuts, -0.22, 0.18) if cuts else 1.0
    entries = jax.random.normal(own_key, shape, jnp.float32) * scale * loudness
    return jnp.minimum(jnp.maximum(entries, -bound), bound).astype(held_as)


def setup_inputs(seed: int = 0) -> dict:
    splits = jax.random.split(jax.random.key(seed), 8)
    return {
        "block_q": draw_block_q(jax.random.fold_in(splits[7], 71), 0),
        "block_kv": normal_values(splits[1], (2, CONTEXT, KVH * HD), 1.0, 6.0, ((1, 8), (2, 4))),
        "lengths": draw_lengths(jax.random.fold_in(splits[7], 71), 0),
        "tenant": jax.random.randint(splits[3], (1,), 0, TENANTS).astype(jnp.int32),
        "prefix_kv": normal_values(splits[4], (2, TENANTS, ANC, KVH * HD), 1.0, 6.0, ((1, 8), (3, 4))),
        "decode_q": draw_decode_q(jax.random.fold_in(splits[7], 71), 0),
        "decode_pos": draw_decode_pos(jax.random.fold_in(splits[7], 71), 0),
    }


MASKED_SCORE = -1e30


def reference(block_q, block_kv, lengths, tenant, prefix_kv, decode_q, decode_pos):
    scale = HD ** -0.5
    group_size = QH // KVH
    anchor = lax.dynamic_index_in_dim(prefix_kv, tenant[0].astype(jnp.int32), 1, keepdims=False)
    anchor_keys = anchor[0].reshape(ANC, KVH, HD).astype(jnp.float32)
    anchor_values = anchor[1].reshape(ANC, KVH, HD).astype(jnp.float32)
    token_index = jnp.arange(BLK, dtype=jnp.int32)
    key_index = jnp.arange(ANC + BLK, dtype=jnp.int32) - ANC

    def prefill_block(element):
        queries, kv_block, length = element
        key_rows = jnp.concatenate([anchor_keys, kv_block[0].reshape(BLK, KVH, HD).astype(jnp.float32)], 0)
        value_rows = jnp.concatenate([anchor_values, kv_block[1].reshape(BLK, KVH, HD).astype(jnp.float32)], 0)
        grouped = queries.reshape(BLK, KVH, group_size, HD).astype(jnp.float32)
        scores = jnp.einsum("qhgd,khd->hgqk", grouped, key_rows) * scale
        visible = (key_index[None, :] < 0) | ((key_index[None, :] <= token_index[:, None]) & (key_index[None, :] < length))
        highest = jnp.max(jnp.where(visible, scores, MASKED_SCORE), axis=-1, keepdims=True)
        weights = jnp.where(visible, jnp.exp(scores - highest), 0.0)
        weight_sum = jnp.sum(weights, axis=-1)
        rounded = lax.optimization_barrier(weights.astype(jnp.bfloat16)).astype(jnp.float32)
        weighted = jnp.einsum("hgqk,khd->qhgd", rounded, value_rows)
        weighted = weighted / jnp.transpose(weight_sum, (2, 0, 1))[..., None]
        weighted = jnp.where(token_index[:, None, None, None] < length, weighted, 0.0)
        return weighted.reshape(BLK, QH * HD).astype(jnp.bfloat16)

    kv_blocks = jnp.transpose(block_kv.reshape(2, BLOCKS, BLK, KVH * HD), (1, 0, 2, 3))
    prefill_out = lax.map(prefill_block, (block_q.reshape(BLOCKS, BLK, QH * HD), kv_blocks, lengths))
    prefill_out = prefill_out.reshape(CONTEXT, QH * HD)

    offsets = (jnp.cumsum(lengths) - lengths).astype(jnp.int32)
    block_pos = (ANC + offsets[:, None] + token_index[None, :]).astype(jnp.int32).reshape(CONTEXT)
    block_ok = (token_index[None, :] < lengths[:, None]).reshape(CONTEXT)
    key_pos = jnp.concatenate([jnp.arange(ANC, dtype=jnp.int32), block_pos], 0)
    key_ok = jnp.concatenate([jnp.ones((ANC,), dtype=bool), block_ok], 0)
    all_keys = jnp.concatenate([anchor[0], block_kv[0]], 0).reshape(ANC + CONTEXT, KVH, HD)
    all_values = jnp.concatenate([anchor[1], block_kv[1]], 0).reshape(ANC + CONTEXT, KVH, HD)
    flat_count = STEPS * QROWS
    limits = decode_pos.reshape(flat_count)
    visible = key_ok[None, :] & (key_pos[None, :] < limits[:, None])
    head_queries = jnp.transpose(decode_q.reshape(flat_count, QH, HD), (1, 0, 2))

    def decode_head(element):
        queries, head_index = element
        kv_slot = head_index // group_size
        key_rows = lax.dynamic_index_in_dim(all_keys, kv_slot, 1, keepdims=False).astype(jnp.float32)
        value_rows = lax.dynamic_index_in_dim(all_values, kv_slot, 1, keepdims=False).astype(jnp.float32)
        scores = jnp.dot(queries.astype(jnp.float32), key_rows.T, preferred_element_type=jnp.float32) * scale
        highest = jnp.max(jnp.where(visible, scores, MASKED_SCORE), axis=-1, keepdims=True)
        weights = jnp.where(visible, jnp.exp(scores - highest), 0.0)
        weight_sum = jnp.sum(weights, axis=-1, keepdims=True)
        rounded = lax.optimization_barrier(weights.astype(jnp.bfloat16)).astype(jnp.float32)
        return jnp.dot(rounded, value_rows, preferred_element_type=jnp.float32) / weight_sum

    decoded = lax.map(decode_head, (head_queries, jnp.arange(QH, dtype=jnp.int32)))
    decode_out = jnp.transpose(decoded, (1, 0, 2)).reshape(STEPS, QROWS, QH * HD).astype(jnp.bfloat16)
    return prefill_out, decode_out
```

```python
import functools
import math

import jax
import jax.numpy as jnp
from jax import lax
from jax.experimental import pallas as pl
from jax.experimental.pallas import tpu as pltpu
from jax.sharding import PartitionSpec as P

HD = 128
MASKED = -1e30
SCALE2 = HD ** (-0.5) * math.log2(math.e)
F32 = jnp.float32
BF16 = jnp.bfloat16


def scores_of(q, k):
    return lax.dot_general(q, k, (((1,), (1,)), ((), ())), preferred_element_type=F32)


def mix(p, v):
    return lax.dot_general(p.astype(BF16), v, (((1,), (0,)), ((), ())), preferred_element_type=F32)


def parts_of(x):
    high = x.astype(BF16)
    rest = x - high.astype(F32)
    middle = rest.astype(BF16)
    low = (rest - middle.astype(F32)).astype(BF16)
    return high.astype(F32), middle.astype(F32), low.astype(F32)


def kernel(
    n, len_ref, pos_ref, q_ref, kv_ref, anchor_ref, dq_ref, out_ref, dout_ref,
    qall, info, psend, precv, q_send, q_recv, i_send, i_recv, p_send, p_recv,
):
    me = lax.axis_index("ctx")
    rows, width = q_ref.shape
    anc = anchor_ref.shape[1]
    groups = kv_ref.shape[2] // HD
    per_group = width // HD // groups
    steps = pos_ref.shape[0]
    drows = steps * per_group
    total = groups * drows
    length = len_ref[0]

    def remote(buffer, slot, to_slot, send, recv, peer):
        return pltpu.make_async_remote_copy(
            src_ref=buffer.at[slot], dst_ref=buffer.at[to_slot],
            send_sem=send, recv_sem=recv,
            device_id={"ctx": peer}, device_id_type=pl.DeviceIdType.MESH,
        )

    def query_copies(peer, source):
        return (
            remote(qall, me, source, q_send.at[peer], q_recv.at[source], peer),
            remote(info, me, source, i_send.at[peer], i_recv.at[source], peer),
        )

    def partial_copy(peer, source):
        return pltpu.make_async_remote_copy(
            src_ref=psend.at[peer], dst_ref=precv.at[source],
            send_sem=p_send.at[peer], recv_sem=p_recv.at[source],
            device_id={"ctx": peer}, device_id_type=pl.DeviceIdType.MESH,
        )

    def peers(act):
        def step(d, carry):
            act(lax.rem(me + d, n))
            return carry
        lax.fori_loop(1, n, step, 0)

    barrier = pltpu.get_barrier_semaphore()
    peers(lambda peer: pl.semaphore_signal(
        barrier, inc=1, device_id={"ctx": peer}, device_id_type=pl.DeviceIdType.MESH))
    qall[me] = dq_ref[...]
    for s in range(steps):
        info[me, s * per_group:(s + 1) * per_group] = jnp.full((per_group, HD), pos_ref[s, 0], jnp.int32)
    info[me, drows:drows + 8] = jnp.full((8, HD), length, jnp.int32)
    pl.semaphore_wait(barrier, n - 1)

    def send_queries(peer):
        for copy in query_copies(peer, me):
            copy.start()

    peers(send_queries)

    row_index = lax.broadcasted_iota(jnp.int32, (rows, rows), 0)
    key_index = lax.broadcasted_iota(jnp.int32, (rows, rows), 1)
    visible = (key_index <= row_index) & (key_index < length)
    kept_row = lax.broadcasted_iota(jnp.int32, (rows, HD), 0) < length

    def prefill_group(g):
        lanes = slice(g * HD, (g + 1) * HD)

        def head(i, carry):
            column = pl.ds(pl.multiple_of((g * per_group + i) * HD, HD), HD)
            q = q_ref[:, column]
            s_a = scores_of(q, anchor_ref[0, :, lanes])
            s_b = jnp.where(visible, scores_of(q, kv_ref[0, :, lanes]), MASKED)
            top = jnp.maximum(
                jnp.max(s_a, axis=1, keepdims=True), jnp.max(s_b, axis=1, keepdims=True))
            w_a = jnp.exp2((s_a - top) * SCALE2)
            w_b = jnp.exp2((s_b - top) * SCALE2)
            weight = jnp.sum(w_a, axis=1, keepdims=True) + jnp.sum(w_b, axis=1, keepdims=True)
            o = mix(w_a, anchor_ref[1, :, lanes]) + mix(w_b, kv_ref[1, :, lanes])
            out_ref[:, column] = jnp.where(kept_row, o * (1.0 / weight), 0.0).astype(BF16)
            return carry

        lax.fori_loop(0, per_group, head, 0)

    prefill_group(0)

    def wait_queries(peer):
        for copy in query_copies(peer, peer):
            copy.wait_recv()

    peers(wait_queries)

    def add_length(source, sum_):
        return sum_ + jnp.where(source < me, info[source, drows:drows + 8], 0)

    offset = lax.fori_loop(0, n, add_length, jnp.zeros((8, HD), jnp.int32))[0:1]
    limit = jnp.minimum(info[:, 0:drows].reshape(n * drows, HD) - (anc + offset), length)
    lane = lax.broadcasted_iota(jnp.int32, (n * drows, HD), 1)
    for g in range(groups):
        lanes = slice(g * HD, (g + 1) * HD)
        q = qall[:, g * drows:(g + 1) * drows].reshape(n * drows, HD)
        s = scores_of(q, kv_ref[0, :, lanes])
        seen = jnp.concatenate([lane + c * HD < limit for c in range(rows // HD)], axis=1)
        s = jnp.where(seen, s, MASKED)
        top = jnp.max(s, axis=1, keepdims=True)
        w = jnp.where(seen, jnp.exp2((s - top) * SCALE2), 0.0)
        weight = jnp.sum(w, axis=1, keepdims=True)
        o = mix(w, kv_ref[1, :, lanes]) * (1.0 / jnp.maximum(weight, 1e-30))
        psend[:, g * drows:(g + 1) * drows] = o.astype(BF16).reshape(n, drows, HD)
        stats = jnp.zeros((n * drows, HD), F32)
        for place, part in enumerate(parts_of(top) + parts_of(weight)):
            stats = jnp.where(lane // 16 == place, part, stats)
        psend[:, total + g * drows:total + (g + 1) * drows] = stats.astype(BF16).reshape(n, drows, HD)
    precv[me] = psend[me]
    peers(lambda peer: partial_copy(peer, me).start())

    for g in range(1, groups):
        prefill_group(g)

    own_limit = info[me, 0:drows]
    own_lane = lax.broadcasted_iota(jnp.int32, (drows, HD), 1)
    anchored = []
    for g in range(groups):
        lanes = slice(g * HD, (g + 1) * HD)
        s = scores_of(dq_ref[g * drows:(g + 1) * drows], anchor_ref[0, :, lanes])
        seen = jnp.concatenate([own_lane + c * HD < own_limit for c in range(anc // HD)], axis=1)
        s = jnp.where(seen, s, MASKED)
        top = jnp.max(s, axis=1, keepdims=True)
        w = jnp.where(seen, jnp.exp2((s - top) * SCALE2), 0.0)
        anchored.append((top, jnp.sum(w, axis=1, keepdims=True), mix(w, anchor_ref[1, :, lanes])))

    peers(lambda peer: partial_copy(peer, peer).wait_recv())
    for g in range(groups):
        def join(source, state):
            top, weight, o = state
            part = precv[source, g * drows:(g + 1) * drows].astype(F32)
            stats = precv[source, total + g * drows:total + (g + 1) * drows].astype(F32)
            part_top = stats[:, 0:1] + stats[:, 16:17] + stats[:, 32:33]
            part_weight = stats[:, 48:49] + stats[:, 64:65] + stats[:, 80:81]
            new_top = jnp.maximum(top, part_top)
            old = jnp.exp2((top - new_top) * SCALE2)
            new = jnp.exp2((part_top - new_top) * SCALE2) * part_weight
            return new_top, weight * old + new, o * old + part * new

        top, weight, o = lax.fori_loop(0, n, join, anchored[g])
        dout_ref[g * drows:(g + 1) * drows] = (o * (1.0 / weight)).astype(BF16)

    def wait_sends(peer):
        for copy in query_copies(peer, me):
            copy.wait_send()
        partial_copy(peer, me).wait_send()

    peers(wait_sends)


def body(n, block_q, block_kv, lengths, tenant, prefix_kv, decode_q, decode_pos):
    rows, width = block_q.shape
    groups = block_kv.shape[2] // HD
    per_group = width // HD // groups
    steps = decode_q.shape[0]
    total = steps * width // HD
    mine = lax.axis_index("ctx") == tenant[0]
    anchor = lax.psum(jnp.where(mine, prefix_kv[:, 0], 0).astype(BF16), "ctx")
    dq = decode_q.reshape(steps, groups, per_group, HD).transpose(1, 0, 2, 3).reshape(total, HD)
    vmem = pl.BlockSpec(memory_space=pltpu.VMEM)
    smem = pl.BlockSpec(memory_space=pltpu.SMEM)
    heads = width // HD
    keys = anchor.shape[1] + rows
    out, dout = pl.pallas_call(
        functools.partial(kernel, n),
        out_shape=(
            jax.ShapeDtypeStruct((rows, width), BF16),
            jax.ShapeDtypeStruct((total, HD), BF16),
        ),
        in_specs=[smem, smem, vmem, vmem, vmem, vmem],
        out_specs=(vmem, vmem),
        scratch_shapes=[
            pltpu.VMEM((n, total, HD), BF16),
            pltpu.VMEM((n, steps * per_group + 8, HD), jnp.int32),
            pltpu.VMEM((n, 2 * total, HD), BF16),
            pltpu.VMEM((n, 2 * total, HD), BF16),
        ] + [pltpu.SemaphoreType.DMA((n,))] * 6,
        compiler_params=pltpu.CompilerParams(
            collective_id=0, has_side_effects=True, vmem_limit_bytes=40 * 1024 * 1024),
        cost_estimate=pl.CostEstimate(
            flops=4 * heads * rows * keys * HD, bytes_accessed=4 * rows * width,
            transcendentals=heads * rows * keys),
        name="star_attention",
    )(lengths, decode_pos, block_q, block_kv, anchor, dq)
    dout = dout.reshape(groups, steps, per_group, HD).transpose(1, 0, 2, 3)
    return out, dout.reshape(steps, 1, width)


def solution(mesh):
    in_specs = (
        P("ctx", "tp"),
        P(None, "ctx", "tp"),
        P("ctx"),
        P(),
        P(None, "ctx", None, "tp"),
        P(None, "ctx", "tp"),
        P(None, "ctx"),
    )
    out_specs = (P("ctx", "tp"), P(None, "ctx", "tp"))
    return jax.shard_map(
        functools.partial(body, mesh.shape["ctx"]),
        mesh=mesh, in_specs=in_specs, out_specs=out_specs, check_vma=False)
```

```python
import functools
import math

import jax
import jax.numpy as jnp
from jax import lax
from jax.experimental import pallas as pl
from jax.experimental.pallas import tpu as pltpu
from jax.sharding import PartitionSpec as P

HD = 128
MASKED = -1e30
SCALE2 = HD ** (-0.5) * math.log2(math.e)
F32 = jnp.float32
BF16 = jnp.bfloat16


def scores_of(q, k):
    return lax.dot_general(q, k, (((1,), (1,)), ((), ())), preferred_element_type=F32)


def mix(p, v):
    return lax.dot_general(p.astype(BF16), v, (((1,), (0,)), ((), ())), preferred_element_type=F32)


def parts_of(x):
    high = x.astype(BF16)
    rest = x - high.astype(F32)
    middle = rest.astype(BF16)
    low = (rest - middle.astype(F32)).astype(BF16)
    return high.astype(F32), middle.astype(F32), low.astype(F32)


def kernel(
    n, len_ref, pos_ref, tenant_ref, q_ref, kv_ref, prefix_ref, dq_ref, out_ref, dout_ref,
    qall, info, psend, precv, y_in, z_out, z_in, anchor,
    q_send, q_recv, i_send, i_recv, p_send, p_recv,
    y_send, y_recv, zr_send, zr_recv, za_send, za_recv, yb_send, yb_recv,
):
    me = lax.axis_index("ctx")
    zs = n // 2
    my_y, my_z = lax.rem(me, 2), me // 2
    partner = my_z * 2 + 1 - my_y
    tenant = tenant_ref[0]
    rows, width = q_ref.shape
    anc = prefix_ref.shape[2]
    piece = anc // zs
    groups = kv_ref.shape[2] // HD
    per_group = width // HD // groups
    steps = pos_ref.shape[0]
    drows = steps * per_group
    total = groups * drows
    length = len_ref[0]

    def remote(buffer, slot, to_slot, send, recv, peer):
        return pltpu.make_async_remote_copy(
            src_ref=buffer.at[slot], dst_ref=buffer.at[to_slot],
            send_sem=send, recv_sem=recv,
            device_id={"ctx": peer}, device_id_type=pl.DeviceIdType.MESH,
        )

    def query_copies(peer, source):
        return (
            remote(qall, me, source, q_send.at[peer], q_recv.at[source], peer),
            remote(info, me, source, i_send.at[peer], i_recv.at[source], peer),
        )

    def partial_copy(peer, source):
        return pltpu.make_async_remote_copy(
            src_ref=psend.at[peer], dst_ref=precv.at[source],
            send_sem=p_send.at[peer], recv_sem=p_recv.at[source],
            device_id={"ctx": peer}, device_id_type=pl.DeviceIdType.MESH,
        )

    def copy_to(src, dst, send, recv, peer):
        return pltpu.make_async_remote_copy(
            src_ref=src, dst_ref=dst, send_sem=send, recv_sem=recv,
            device_id={"ctx": peer}, device_id_type=pl.DeviceIdType.MESH,
        )

    def pieces(z):
        return pl.ds(pl.multiple_of(z * piece, piece), piece)

    def half_out(g):
        return copy_to(
            prefix_ref.at[1 - my_y, 0, :, g * HD:(g + 1) * HD], y_in.at[g],
            y_send.at[g], y_recv.at[g], partner)

    def piece_out(g, z, source):
        return copy_to(
            z_out.at[g, pieces(z)], z_in[g].at[source],
            zr_send.at[g, z], zr_recv.at[g, source], z * 2 + my_y)

    def chosen_out(g, z, source):
        rows_ = anchor.at[g, my_y, pieces(source)]
        return copy_to(
            rows_, rows_, za_send.at[g, z], za_recv.at[g, source], z * 2 + my_y)

    def half_back(g, half, z):
        rows_ = anchor.at[g, half, pieces(z)]
        return copy_to(rows_, rows_, yb_send.at[g, z], yb_recv.at[g, z], partner)

    def line(act):
        def step(d, carry):
            act(lax.rem(my_z + d, zs))
            return carry
        lax.fori_loop(1, zs, step, 0)

    def scatter(g):
        half_out(g).wait_recv()
        held = jnp.full((anc, HD), jnp.where(tenant == me, 1, 0), jnp.int32) > 0
        own = prefix_ref[my_y, 0, :, g * HD:(g + 1) * HD].astype(F32)
        z_out[g] = jnp.where(held, own, y_in[g].astype(F32)).astype(BF16)
        line(lambda z: piece_out(g, z, my_z).start())
        z_in[g][my_z] = z_out[g, pieces(my_z)]

    def gather(g):
        line(lambda z: piece_out(g, z, z).wait_recv())
        anchor[g, my_y, pieces(my_z)] = z_in[g][tenant // 2]
        line(lambda z: chosen_out(g, z, my_z).start())
        half_back(g, my_y, my_z).start()

    def hand_back(g):
        def forward(z):
            chosen_out(g, z, z).wait_recv()
            half_back(g, my_y, z).start()
        line(forward)

    def arrive(g):
        lax.fori_loop(0, zs, lambda z, c: (half_back(g, 1 - my_y, z).wait_recv(), c)[1], 0)

    def finish(g):
        half_out(g).wait_send()
        line(lambda z: piece_out(g, z, my_z).wait_send())
        line(lambda z: chosen_out(g, z, my_z).wait_send())
        lax.fori_loop(0, zs, lambda z, c: (half_back(g, my_y, z).wait_send(), c)[1], 0)

    def peers(act):
        def step(d, carry):
            act(lax.rem(me + d, n))
            return carry
        lax.fori_loop(1, n, step, 0)

    barrier = pltpu.get_barrier_semaphore()
    peers(lambda peer: pl.semaphore_signal(
        barrier, inc=1, device_id={"ctx": peer}, device_id_type=pl.DeviceIdType.MESH))
    qall[me] = dq_ref[...]
    for s in range(steps):
        info[me, s * per_group:(s + 1) * per_group] = jnp.full((per_group, HD), pos_ref[s, 0], jnp.int32)
    info[me, drows:drows + 8] = jnp.full((8, HD), length, jnp.int32)
    pl.semaphore_wait(barrier, n - 1)

    def send_queries(peer):
        for copy in query_copies(peer, me):
            copy.start()

    half_out(0).start()
    peers(send_queries)
    for g in range(1, groups):
        half_out(g).start()

    row_index = lax.broadcasted_iota(jnp.int32, (rows, rows), 0)
    key_index = lax.broadcasted_iota(jnp.int32, (rows, rows), 1)
    visible = (key_index <= row_index) & (key_index < length)
    kept_row = lax.broadcasted_iota(jnp.int32, (rows, HD), 0) < length

    def prefill_group(g):
        lanes = slice(g * HD, (g + 1) * HD)

        def one(i):
            column = pl.ds(pl.multiple_of((g * per_group + i) * HD, HD), HD)
            q = q_ref[:, column]
            s_a = scores_of(q, anchor[g, 0])
            s_b = jnp.where(visible, scores_of(q, kv_ref[0, :, lanes]), MASKED)
            top = jnp.maximum(
                jnp.max(s_a, axis=1, keepdims=True), jnp.max(s_b, axis=1, keepdims=True))
            w_a = jnp.exp2((s_a - top) * SCALE2)
            w_b = jnp.exp2((s_b - top) * SCALE2)
            weight = jnp.sum(w_a, axis=1, keepdims=True) + jnp.sum(w_b, axis=1, keepdims=True)
            o = mix(w_a, anchor[g, 1]) + mix(w_b, kv_ref[1, :, lanes])
            out_ref[:, column] = jnp.where(kept_row, o * (1.0 / weight), 0.0).astype(BF16)

        def heads(i, carry):
            one(2 * i)
            one(2 * i + 1)
            return carry

        lax.fori_loop(0, per_group // 2, heads, 0)

    def wait_queries(peer):
        for copy in query_copies(peer, peer):
            copy.wait_recv()

    scatter(0)
    peers(wait_queries)

    def add_length(source, sum_):
        return sum_ + jnp.where(source < me, info[source, drows:drows + 8], 0)

    offset = lax.fori_loop(0, n, add_length, jnp.zeros((8, HD), jnp.int32))[0:1]
    limit = jnp.minimum(info[:, 0:drows].reshape(n * drows, HD) - (anc + offset), length)
    lane = lax.broadcasted_iota(jnp.int32, (n * drows, HD), 1)
    for g in range(groups):
        lanes = slice(g * HD, (g + 1) * HD)
        q = qall[:, g * drows:(g + 1) * drows].reshape(n * drows, HD)
        s = scores_of(q, kv_ref[0, :, lanes])
        seen = jnp.concatenate([lane + c * HD < limit for c in range(rows // HD)], axis=1)
        s = jnp.where(seen, s, MASKED)
        top = jnp.max(s, axis=1, keepdims=True)
        w = jnp.where(seen, jnp.exp2((s - top) * SCALE2), 0.0)
        weight = jnp.sum(w, axis=1, keepdims=True)
        o = mix(w, kv_ref[1, :, lanes]) * (1.0 / jnp.maximum(weight, 1e-30))
        psend[:, g * drows:(g + 1) * drows] = o.astype(BF16).reshape(n, drows, HD)
        stats = jnp.zeros((n * drows, HD), F32)
        for place, part in enumerate(parts_of(top) + parts_of(weight)):
            stats = jnp.where(lane // 16 == place, part, stats)
        psend[:, total + g * drows:total + (g + 1) * drows] = stats.astype(BF16).reshape(n, drows, HD)
    precv[me] = psend[me]
    peers(lambda peer: partial_copy(peer, me).start())

    for g in range(1, groups):
        scatter(g)
    for g in range(groups):
        gather(g)
    for g in range(groups):
        hand_back(g)
    for g in range(groups):
        arrive(g)
        prefill_group(g)

    own_limit = info[me, 0:drows]
    own_lane = lax.broadcasted_iota(jnp.int32, (drows, HD), 1)
    anchored = []
    for g in range(groups):
        s = scores_of(dq_ref[g * drows:(g + 1) * drows], anchor[g, 0])
        seen = jnp.concatenate([own_lane + c * HD < own_limit for c in range(anc // HD)], axis=1)
        s = jnp.where(seen, s, MASKED)
        top = jnp.max(s, axis=1, keepdims=True)
        w = jnp.where(seen, jnp.exp2((s - top) * SCALE2), 0.0)
        anchored.append((top, jnp.sum(w, axis=1, keepdims=True), mix(w, anchor[g, 1])))

    peers(lambda peer: partial_copy(peer, peer).wait_recv())
    for g in range(groups):
        def join(source, state):
            top, weight, o = state
            part = precv[source, g * drows:(g + 1) * drows].astype(F32)
            stats = precv[source, total + g * drows:total + (g + 1) * drows].astype(F32)
            part_top = stats[:, 0:1] + stats[:, 16:17] + stats[:, 32:33]
            part_weight = stats[:, 48:49] + stats[:, 64:65] + stats[:, 80:81]
            new_top = jnp.maximum(top, part_top)
            old = jnp.exp2((top - new_top) * SCALE2)
            new = jnp.exp2((part_top - new_top) * SCALE2) * part_weight
            return new_top, weight * old + new, o * old + part * new

        top, weight, o = lax.fori_loop(0, n, join, anchored[g])
        dout_ref[g * drows:(g + 1) * drows] = (o * (1.0 / weight)).astype(BF16)

    def wait_sends(peer):
        for copy in query_copies(peer, me):
            copy.wait_send()
        partial_copy(peer, me).wait_send()

    peers(wait_sends)
    for g in range(groups):
        finish(g)


def body(n, block_q, block_kv, lengths, tenant, prefix_kv, decode_q, decode_pos):
    rows, width = block_q.shape
    groups = block_kv.shape[2] // HD
    per_group = width // HD // groups
    steps = decode_q.shape[0]
    total = steps * width // HD
    dq = decode_q.reshape(steps, groups, per_group, HD).transpose(1, 0, 2, 3).reshape(total, HD)
    vmem = pl.BlockSpec(memory_space=pltpu.VMEM)
    smem = pl.BlockSpec(memory_space=pltpu.SMEM)
    heads = width // HD
    anc = prefix_kv.shape[2]
    zs = n // 2
    keys = anc + rows
    out, dout = pl.pallas_call(
        functools.partial(kernel, n),
        out_shape=(
            jax.ShapeDtypeStruct((rows, width), BF16),
            jax.ShapeDtypeStruct((total, HD), BF16),
        ),
        in_specs=[smem, smem, smem, vmem, vmem, vmem, vmem],
        out_specs=(vmem, vmem),
        scratch_shapes=[
            pltpu.VMEM((n, total, HD), BF16),
            pltpu.VMEM((n, steps * per_group + 8, HD), jnp.int32),
            pltpu.VMEM((n, 2 * total, HD), BF16),
            pltpu.VMEM((n, 2 * total, HD), BF16),
            pltpu.VMEM((groups, anc, HD), BF16),
            pltpu.VMEM((groups, anc, HD), BF16),
            [pltpu.VMEM((zs, anc // zs, HD), BF16)] * groups,
            pltpu.VMEM((groups, 2, anc, HD), BF16),
        ] + [pltpu.SemaphoreType.DMA((n,))] * 6
        + [pltpu.SemaphoreType.DMA((groups,))] * 2
        + [pltpu.SemaphoreType.DMA((groups, zs))] * 6,
        compiler_params=pltpu.CompilerParams(
            collective_id=0, has_side_effects=True, vmem_limit_bytes=40 * 1024 * 1024),
        cost_estimate=pl.CostEstimate(
            flops=4 * heads * rows * keys * HD, bytes_accessed=4 * rows * width,
            transcendentals=heads * rows * keys),
        name="star_attention",
    )(lengths, decode_pos, tenant, block_q, block_kv, prefix_kv, dq)
    dout = dout.reshape(groups, steps, per_group, HD).transpose(1, 0, 2, 3)
    return out, dout.reshape(steps, 1, width)


def solution(mesh):
    in_specs = (
        P("ctx", "tp"),
        P(None, "ctx", "tp"),
        P("ctx"),
        P(),
        P(None, "ctx", None, "tp"),
        P(None, "ctx", "tp"),
        P(None, "ctx"),
    )
    out_specs = (P("ctx", "tp"), P(None, "ctx", "tp"))
    return jax.shard_map(
        functools.partial(body, mesh.shape["ctx"]),
        mesh=mesh, in_specs=in_specs, out_specs=out_specs, check_vma=False)
```
